512 devices in a mesh: row: 16 (over x, z_lo), col: 32 (over z_hi, y, core).
Axes of the slice: x: 4, y: 4, z: 16 (z_hi: 4, z_lo: 4; z = z_hi * 4 + z_lo), core: 2. Of those that a mesh axis runs over, the one named last changes fastest.
Arguments:
- left_vals: bfloat16 [12288, 4096], P('row', 'col'), may hold values from -6 to 6
- left_scale: float32 [96, 32], P('row', 'col'), may hold values from 0.02 to 0.2
- left_keep: int32 [96, 32], P('row', 'col'), may hold values 0 or 1
- right_vals: bfloat16 [4096, 24576], P('row', 'col'), may hold values from -6 to 6
- right_scale: float32 [32, 192], P('row', 'col'), may hold values from 0.02 to 0.35, as said below
- right_keep: int32 [32, 192], P('row', 'col'), may hold values 0 or 1
- result_keep: int32 [96, 192], P('row', 'col'), may hold values 0 or 1
Outputs:
- flow: float32 [12288, 24576], P('row', 'col')
The draws below stay inside these ranges and needn't reach their ends.
Inputs may be any that keep to these rules, and one draw needn't show every extreme that they name: `right_scale`: each tile's scale, positive.
All inputs are finite; a program needn't handle non-finite values. No bound on the sum of `left_keep` or of `right_keep` or of `result_keep` on one device may be relied on, other than what follows from the above.
Results may differ from the reference program's by a relative error of at most 0.0047.
Values may be sent and summed in bfloat16 or wider, within the bound.
No kernel may reach another device: no remote copies, remote signals or barrier semaphores. Data moves between devices by JAX's collectives and lax.ppermute only.
A program may use at most 64 MiB of HBM per device.

```python
import math
import jax
import jax.numpy as jnp
from jax import lax

TILE = 128
KT = 32
NT_DEV = 6
MT = 96
NT = 192
N_COL = 32


def draw_right_scale(key, part):
    key = jax.random.fold_in(key, 7)
    cols = NT_DEV * N_COL
    position = jnp.arange(cols, dtype=jnp.float32) / max(cols - 1, 1)
    rising = jnp.sqrt(1.0 + 2.0 * position)
    base = jnp.exp(jax.random.uniform(key, (KT, cols), jnp.float32, jnp.log(0.03), jnp.log(0.15)))
    return base * rising[None, :]


def plant(values, stream_key, least, largest):
    longest = values.shape.index(max(values.shape))
    spots = []
    for shift in (0, 1):
        where = [jax.random.randint(jax.random.fold_in(stream_key, axis), (), 0, length) for axis, length in enumerate(values.shape)]
        where[longest] = (where[longest] + shift) % values.shape[longest]
        spots.append(tuple(where))
    return values.at[spots[0]].set(least).at[spots[1]].set(largest)


def level_of(stream_key, shape, shards, least, largest):
    def one(dim, parts):
        draws = jax.random.uniform(jax.random.fold_in(jax.random.fold_in(stream_key, 6), dim), (parts,), jnp.float32, least / len(shards), largest / len(shards))
        return jnp.repeat(jnp.exp(draws), shape[dim] // parts).reshape((-1,) + (1,) * (len(shape) - dim - 1))

    loudness = one(*shards[0])
    for cut in shards[1:]:
        loudness = loudness * one(*cut)
    return loudness


def normal_values(own_key, dims, deviation, reach, cuts=(), held_as=jnp.bfloat16):
    array = jax.random.normal(own_key, dims, jnp.float32) * deviation
    if len(cuts) > 0:
        array = level_of(own_key, dims, cuts, -0.22, 0.18) * array
    return jnp.clip(array, min=-reach, max=reach).astype(held_as)


def setup_inputs(seed: int = 0) -> dict:
    key_list = jax.random.split(jax.random.key(seed), 8)
    left_vals = normal_values(key_list[0], (MT * TILE, KT * TILE), 1.0, 6.0, ((0, 16), (1, 32)))
    left_scale = jnp.clip(jnp.exp(math.log(0.2) - 2.3025851 * jax.random.uniform(key_list[1], (MT, KT), jnp.float32) ** level_of(key_list[1], (MT, KT), ((0, 16), (1, 32)), -0.2, 0.2)), 0.02, 0.2)
    left_keep = plant((jax.random.randint(key_list[2], (MT, KT), 0, 4) < 3).astype(jnp.int32), jax.random.fold_in(key_list[2], 1), 0, 1)
    right_vals = normal_values(key_list[3], (KT * TILE, NT * TILE), 1.0, 6.0, ((0, 16), (1, 32)))
    right_scale = draw_right_scale(jax.random.fold_in(key_list[7], 71), 0)
    right_keep = plant((jax.random.randint(key_list[5], (KT, NT), 0, 4) < 3).astype(jnp.int32), jax.random.fold_in(key_list[5], 1), 0, 1)
    result_keep = plant((jax.random.randint(key_list[6], (MT, NT), 0, 2) < 1).astype(jnp.int32), jax.random.fold_in(key_list[6], 1), 0, 1)
    return {"left_vals": left_vals, "left_scale": left_scale, "left_keep": left_keep, "right_vals": right_vals, "right_scale": right_scale, "right_keep": right_keep, "result_keep": result_keep}


def tiled(values, scales, keep):
    rows, cols = scales.shape
    size = values.shape[0] // rows
    factor = scales * keep.astype(jnp.float32)
    shaped = values.astype(jnp.float32).reshape(rows, size, cols, size) * factor[:, None, :, None]
    return shaped.reshape(values.shape).astype(jnp.bfloat16)


def reference(left_vals, left_scale, left_keep, right_vals, right_scale, right_keep, result_keep):
    left_tiles = tiled(left_vals, left_scale, left_keep)
    right_tiles = tiled(right_vals, right_scale, right_keep)
    width = NT * TILE

    def one_block(index):
        rows = lax.dynamic_slice_in_dim(left_tiles, index * TILE, TILE, 0)
        product = jnp.dot(rows, right_tiles, preferred_element_type=jnp.float32)
        keep_row = lax.dynamic_slice_in_dim(result_keep, index, 1, 0).astype(jnp.float32)
        keep_cols = jnp.repeat(keep_row[0], TILE)
        pruned = product * product * keep_cols[None, :]
        totals = jnp.sum(pruned, axis=1, keepdims=True)
        return width * pruned / (totals + 1e-6)

    blocks = lax.map(one_block, jnp.arange(MT, dtype=jnp.int32))
    return blocks.reshape(MT * TILE, width)
```

```python
import jax
import jax.numpy as jnp
from jax import lax
from jax.experimental import pallas as pl
from jax.experimental.pallas import tpu as pltpu
from jax.sharding import Mesh, PartitionSpec as P

AXES = ("x", "zl", "zh", "y", "core")
SIDE = 4
TILE = 128


def tiled(values, scales, keep):
    rows, cols = scales.shape
    size = values.shape[0] // rows
    factor = scales * keep.astype(jnp.float32)
    shaped = values.astype(jnp.float32).reshape(rows, size, cols, size) * factor[:, None, :, None]
    return shaped.reshape(values.shape).astype(jnp.bfloat16)


def step(value, axis):
    pairs = []
    for i in range(SIDE):
        pairs.append((2 * i, 2 * ((i + 1) % SIDE)))
        pairs.append((2 * i + 1, 2 * ((i - 1) % SIDE) + 1))
    return lax.ppermute(value, (axis, "core"), pairs)


def ring(value, axis):
    blocks = [value]
    for _ in range(SIDE - 1):
        blocks.append(step(blocks[-1], axis))
    return blocks


def multiply(place_ref, keep_ref, own_ref, other_ref, *refs):
    count = SIDE * SIDE
    right_refs = refs[:count]
    pruned_ref, total_ref, left, right, left_sem, right_sem = refs[count:]
    depth = right_refs[0].shape[0]
    half = own_ref.shape[2]
    copies = []
    for i in range(count):
        at = pl.multiple_of(place_ref[i] * half, half)
        copies.append(pltpu.make_async_copy(own_ref.at[i], left.at[:, pl.ds(at, half)], left_sem))
        at = pl.multiple_of(place_ref[count + i] * half, half)
        copies.append(pltpu.make_async_copy(other_ref.at[i], left.at[:, pl.ds(at, half)], left_sem))
        at = pl.multiple_of(place_ref[2 * count + i] * depth, depth)
        copies.append(pltpu.make_async_copy(right_refs[i], right.at[pl.ds(at, depth), :], right_sem))
    for copy in copies:
        copy.start()
    for copy in copies:
        copy.wait()
    rows = 2 * TILE
    for m in range(left.shape[0] // rows):
        product = jnp.dot(left[m * rows:(m + 1) * rows, :], right[...], preferred_element_type=jnp.float32)
        for r in range(rows // TILE):
            total = jnp.zeros((TILE, TILE), jnp.float32)
            at = m * rows + r * TILE
            for n in range(right.shape[1] // TILE):
                block = product[r * TILE:(r + 1) * TILE, n * TILE:(n + 1) * TILE]
                block = block * block * keep_ref[at // TILE, n].astype(jnp.float32)
                pruned_ref[at:at + TILE, n * TILE:(n + 1) * TILE] = block
                total = total + block
            total_ref[at:at + TILE, :] = jnp.sum(total, axis=1, keepdims=True)


def per_device(left_vals, left_scale, left_keep, right_vals, right_scale, right_keep, result_keep):
    x, zl, zh, y, core = (lax.axis_index(a) for a in AXES)
    way = 1 - 2 * core
    right_tiles = tiled(right_vals, right_scale, right_keep)
    left_tiles = tiled(left_vals, left_scale, left_keep)

    right_blocks, right_place = [], []
    for k, lane in enumerate(ring(right_tiles, "zl")):
        for s, block in enumerate(ring(lane, "x")):
            right_blocks.append(block)
            right_place.append((x - s * way) % SIDE * SIDE + (zl - k * way) % SIDE)
    left_blocks, own_place, other_place = [], [], []
    for k, lane in enumerate(ring(left_tiles, "zh")):
        for s, block in enumerate(ring(lane, "y")):
            left_blocks.append(block)
            own_place.append(((zh - k * way) % SIDE * SIDE + (y - s * way) % SIDE) * 2 + core)
            other_place.append(((zh + k * way) % SIDE * SIDE + (y + s * way) % SIDE) * 2 + 1 - core)
    own = jnp.stack(left_blocks)
    other = lax.ppermute(own, "core", [(0, 1), (1, 0)])
    place = jnp.stack(own_place + other_place + right_place).astype(jnp.int32)

    rows, cols = left_vals.shape[0], right_vals.shape[1]
    depth = right_vals.shape[0] * SIDE * SIDE
    smem = pl.BlockSpec(memory_space=pltpu.SMEM)
    vmem = pl.BlockSpec(memory_space=pltpu.VMEM)
    hbm = pl.BlockSpec(memory_space=pl.ANY)
    pruned, partial_totals = pl.pallas_call(
        multiply,
        out_shape=(
            jax.ShapeDtypeStruct((rows, cols), jnp.float32),
            jax.ShapeDtypeStruct((rows, 1), jnp.float32),
        ),
        in_specs=[smem, smem, hbm, hbm] + [hbm] * len(right_blocks),
        out_specs=(vmem, vmem),
        scratch_shapes=[
            pltpu.VMEM((rows, depth), jnp.bfloat16),
            pltpu.VMEM((depth, cols), jnp.bfloat16),
            pltpu.SemaphoreType.DMA,
            pltpu.SemaphoreType.DMA,
        ],
        compiler_params=pltpu.CompilerParams(vmem_limit_bytes=32 * 1024 * 1024),
    )(place, result_keep, own, other, *right_blocks)
    totals = partial_totals
    for axis in ("core", "y", "zh"):
        totals = lax.psum(totals, axis)
    width = cols * lax.axis_size("zh") * lax.axis_size("y") * lax.axis_size("core")
    return width * pruned / (totals + 1e-06)


def solution(mesh):
    fine = Mesh(mesh.devices.reshape(SIDE, SIDE, SIDE, SIDE, 2), AXES)
    spec = P(("x", "zl"), ("zh", "y", "core"))
    return jax.shard_map(
        per_device,
        mesh=fine,
        in_specs=(spec,) * 7,
        out_specs=spec,
        check_vma=False,
    )
```

```python
import functools

import jax
import jax.numpy as jnp
from jax import lax
from jax.experimental import pallas as pl
from jax.experimental.pallas import tpu as pltpu
from jax.sharding import Mesh, PartitionSpec as P

AXES = ("x", "zl", "zh", "y", "core")
SIDE = 4
TILE = 128
MIB = 1024 * 1024
VMEM = pl.BlockSpec(memory_space=pltpu.VMEM)
SMEM = pl.BlockSpec(memory_space=pltpu.SMEM)
ANY = pl.BlockSpec(memory_space=pl.ANY)


def step(value, axis, by=1):
    pairs = []
    for i in range(SIDE):
        pairs.append((2 * i, 2 * ((i + by) % SIDE)))
        pairs.append((2 * i + 1, 2 * ((i - by) % SIDE) + 1))
    return lax.ppermute(value, (axis, "core"), pairs)


def swap(value):
    return lax.ppermute(value, "core", [(0, 1), (1, 0)])


def copy_parts(count, *refs):
    at = 0
    for ref in refs[:count]:
        refs[-1][at:at + ref.shape[0]] = ref[...]
        at += ref.shape[0]


def join(parts, after=()):
    shape = (sum(p.shape[0] for p in parts),) + parts[0].shape[1:]
    return pl.pallas_call(
        functools.partial(copy_parts, len(parts)),
        out_shape=jax.ShapeDtypeStruct(shape, jnp.bfloat16),
        in_specs=[VMEM] * (len(parts) + len(after)),
        out_specs=VMEM,
        compiler_params=pltpu.CompilerParams(vmem_limit_bytes=8 * MIB),
    )(*parts, *after)


def scale_tiles(*refs):
    given, made, held, sems = refs[:6], refs[6:8], refs[8:14], refs[14]
    copies = [pltpu.make_async_copy(given[i], held[i], sems.at[i]) for i in range(6)]
    for copy in copies:
        copy.start()
    for side in range(2):
        for copy in copies[3 * side:3 * side + 3]:
            copy.wait()
        scale_ref, keep_ref, values_ref = held[3 * side:3 * side + 3]
        factors = scale_ref[...] * keep_ref[...].astype(jnp.float32)
        rows, cols = (n // TILE for n in values_ref.shape)
        for i in range(rows):
            for j in range(cols):
                at = (slice(i * TILE, (i + 1) * TILE), slice(j * TILE, (j + 1) * TILE))
                factor = factors[i:i + 1, j:j + 1] if cols > 1 else factors[0:1, i:i + 1]
                made[side][at] = (values_ref[at].astype(jnp.float32) * factor).astype(jnp.bfloat16)


def tiled(*operands):
    return pl.pallas_call(
        scale_tiles,
        out_shape=[jax.ShapeDtypeStruct(operands[i].shape, jnp.bfloat16) for i in (2, 5)],
        in_specs=[pl.BlockSpec(memory_space=pl.ANY)] * 6,
        out_specs=[VMEM] * 2,
        scratch_shapes=[pltpu.VMEM(v.shape, v.dtype) for v in operands] + [pltpu.SemaphoreType.DMA((6,))],
        compiler_params=pltpu.CompilerParams(vmem_limit_bytes=60 * MIB),
    )(*operands)


def multiply(left_at, right_at, at_ref, keep_ref, *refs):
    left_refs, refs = refs[:len(left_at)], refs[len(left_at):]
    right_refs, refs = refs[:len(right_at)], refs[len(right_at):]
    pruned_ref, total_ref, left, right = refs
    x, zl, zh, y, core = (at_ref[i] for i in range(5))
    way = 1 - 2 * core

    def left_place(first, lanes, first_step, sign, i):
        k, s = first + lax.rem(i, lanes), first_step + lax.div(i, lanes)
        block = lax.rem(zh - k * sign * way + SIDE, SIDE) * SIDE + lax.rem(y - s * sign * way + SIDE, SIDE)
        return block * 2 + (core if sign > 0 else 1 - core)

    def right_place(first, lanes, first_step, i):
        k, s = first + lax.rem(i, lanes), first_step + lax.div(i, lanes)
        return lax.rem(x - s * way + SIDE, SIDE) * SIDE + lax.rem(zl - k * way + SIDE, SIDE)

    for held, place, places, given in ((left, left_place, left_at, left_refs), (right, right_place, right_at, right_refs)):
        for ref, at in zip(given, places):
            def put(i, carry, held=held, place=place, ref=ref, at=at):
                held[place(*at, i)] = ref[i]
                return carry

            lax.fori_loop(0, ref.shape[0], put, 0)
    blocks, rows = left.shape[0], 2 * TILE
    cols = right.shape[2]
    for m in range(left.shape[1] // rows):
        lhs = jnp.concatenate([left[k, m * rows:(m + 1) * rows, :] for k in range(blocks)], axis=1)
        product = jnp.dot(lhs, right[...].reshape(blocks * TILE, cols), preferred_element_type=jnp.float32)
        for r in range(rows // TILE):
            total = jnp.zeros((TILE, TILE), jnp.float32)
            i = m * (rows // TILE) + r
            for n in range(cols // TILE):
                block = product[r * TILE:(r + 1) * TILE, n * TILE:(n + 1) * TILE]
                block = block * block * keep_ref[i, n].astype(jnp.float32)
                pruned_ref[i * TILE:(i + 1) * TILE, n * TILE:(n + 1) * TILE] = block
                total = total + block
            total_ref[i:i + 1, :] = jnp.sum(total.T, axis=0, keepdims=True)


def per_device(left_vals, left_scale, left_keep, right_vals, right_scale, right_keep, result_keep):
    at = jnp.stack([lax.axis_index(a) for a in AXES]).astype(jnp.int32)
    rows, cols = left_vals.shape[0], right_vals.shape[1]
    right_tiles, left_tiles = tiled(
        right_scale, right_keep, right_vals, left_scale.reshape(1, -1), left_keep.reshape(1, -1), left_vals
    )
    z0, h0 = right_tiles[None], left_tiles[None]

    high, lane = [h0], [z0]
    for _ in range(SIDE - 1):
        high.append(step(high[-1], "zh"))
        lane.append(step(lane[-1], "zl"))
    lefts, rights = [], []
    for first in (0, 2):
        own = [join(high[first:first + 2])]
        for _ in range(SIDE - 1):
            own.append(step(own[-1], "y"))
        own = join(own)
        lefts.append((own, (first, 2, 0, 1)))
        lefts.append((swap(own), (first, 2, 0, -1)))
    for first in (0, 2):
        block = join(lane[first:first + 2])
        rights.append((block, (first, 2, 0)))
        for s in range(1, SIDE):
            block = step(block, "x")
            rights.append((block, (first, 2, s)))
    operands = [v for v, _ in lefts + rights]
    pruned, totals = pl.pallas_call(
        functools.partial(multiply, [p for _, p in lefts], [p for _, p in rights]),
        out_shape=(
            jax.ShapeDtypeStruct((rows, cols), jnp.float32),
            jax.ShapeDtypeStruct((rows // TILE, TILE), jnp.float32),
        ),
        in_specs=[SMEM, SMEM] + [VMEM] * len(operands),
        out_specs=(VMEM, VMEM),
        scratch_shapes=[
            pltpu.VMEM((2 * SIDE * SIDE, rows, TILE), jnp.bfloat16),
            pltpu.VMEM((SIDE * SIDE,) + right_vals.shape, jnp.bfloat16),
        ],
        compiler_params=pltpu.CompilerParams(vmem_limit_bytes=52 * MIB),
    )(at, result_keep, *operands)
    totals = totals.reshape(rows)
    for axis in ("core", "y", "zh"):
        totals = lax.psum(totals, axis)
    width = cols * lax.axis_size("zh") * lax.axis_size("y") * lax.axis_size("core")
    return width * pruned / (totals[:, None] + 1e-06)


def solution(mesh):
    fine = Mesh(mesh.devices.reshape(SIDE, SIDE, SIDE, SIDE, 2), AXES)
    spec = P(("x", "zl"), ("zh", "y", "core"))
    return jax.shard_map(
        per_device,
        mesh=fine,
        in_specs=(spec,) * 7,
        out_specs=spec,
        check_vma=False,
    )
```

```python
import functools

import jax
import jax.numpy as jnp
from jax import lax
from jax.experimental import pallas as pl
from jax.experimental.pallas import tpu as pltpu
from jax.sharding import Mesh, PartitionSpec as P

AXES = ("x", "zl", "zh", "y", "core")
SIDE = 4
TILE = 128
MIB = 1024 * 1024
VMEM = pl.BlockSpec(memory_space=pltpu.VMEM)
SMEM = pl.BlockSpec(memory_space=pltpu.SMEM)
ANY = pl.BlockSpec(memory_space=pl.ANY)


def step(value, axis, by=1):
    pairs = []
    for i in range(SIDE):
        pairs.append((2 * i, 2 * ((i + by) % SIDE)))
        pairs.append((2 * i + 1, 2 * ((i - by) % SIDE) + 1))
    return lax.ppermute(value, (axis, "core"), pairs)


def swap(value):
    return lax.ppermute(value, "core", [(0, 1), (1, 0)])


def copy_parts(count, *refs):
    at = 0
    for ref in refs[:count]:
        refs[-1][at:at + ref.shape[0]] = ref[...]
        at += ref.shape[0]


def join(parts, after=()):
    shape = (sum(p.shape[0] for p in parts),) + parts[0].shape[1:]
    return pl.pallas_call(
        functools.partial(copy_parts, len(parts)),
        out_shape=jax.ShapeDtypeStruct(shape, jnp.bfloat16),
        in_specs=[VMEM] * (len(parts) + len(after)),
        out_specs=VMEM,
        compiler_params=pltpu.CompilerParams(vmem_limit_bytes=10 * MIB),
    )(*parts, *after)


def scale_tiles(*refs):
    given, made, held, sems = refs[:6], refs[6:8], refs[8:14], refs[14]
    copies = [pltpu.make_async_copy(given[i], held[i], sems.at[i]) for i in range(6)]
    for copy in copies:
        copy.start()
    for side in range(2):
        for copy in copies[3 * side:3 * side + 3]:
            copy.wait()
        scale_ref, keep_ref, values_ref = held[3 * side:3 * side + 3]
        factors = scale_ref[...] * keep_ref[...].astype(jnp.float32)
        rows, cols = (n // TILE for n in values_ref.shape)
        for i in range(rows):
            for j in range(cols):
                at = (slice(i * TILE, (i + 1) * TILE), slice(j * TILE, (j + 1) * TILE))
                factor = factors[i:i + 1, j:j + 1] if cols > 1 else factors[0:1, i:i + 1]
                made[side][at] = (values_ref[at].astype(jnp.float32) * factor).astype(jnp.bfloat16)


def tiled(*operands):
    return pl.pallas_call(
        scale_tiles,
        out_shape=[jax.ShapeDtypeStruct(operands[i].shape, jnp.bfloat16) for i in (2, 5)],
        in_specs=[pl.BlockSpec(memory_space=pl.ANY)] * 6,
        out_specs=[VMEM] * 2,
        scratch_shapes=[pltpu.VMEM(v.shape, v.dtype) for v in operands] + [pltpu.SemaphoreType.DMA((6,))],
        compiler_params=pltpu.CompilerParams(vmem_limit_bytes=60 * MIB),
    )(*operands)


def multiply(left_at, at_ref, keep_ref, *refs):
    left_refs, right_refs = refs[:len(left_at)], refs[len(left_at):-3]
    pruned_ref, total_ref, left = refs[-3:]
    x, zl, zh, y, core = (at_ref[i] for i in range(5))
    way = 1 - 2 * core

    for ref, (first, lanes, sign) in zip(left_refs, left_at):
        def put(i, carry, ref=ref, first=first, lanes=lanes, sign=sign):
            k, s = first + lax.rem(i, lanes), lax.div(i, lanes)
            across = lax.rem((x - zh + k * sign * way) * way + 4 * SIDE, SIDE)
            along = lax.rem((zl - y + s * sign * way) * way + 4 * SIDE, SIDE)
            block = lax.div(along, 2) * (2 * SIDE) + across * 2 + lax.rem(along, 2)
            left[block * 2 + (core if sign > 0 else 1 - core)] = ref[i]
            return carry

        lax.fori_loop(0, ref.shape[0], put, 0)
    rows, depth, cols = 2 * TILE, right_refs[0].shape[1], right_refs[0].shape[2]
    for m in range(left.shape[1] // rows):
        product, at = None, 0
        for ref in right_refs:
            count = ref.shape[0] * depth // TILE
            lhs = jnp.concatenate([left[k, m * rows:(m + 1) * rows, :] for k in range(at, at + count)], axis=1)
            part = jnp.dot(lhs, ref[...].reshape(-1, cols), preferred_element_type=jnp.float32)
            product = part if product is None else product + part
            at += count
        for r in range(rows // TILE):
            total = jnp.zeros((TILE, TILE), jnp.float32)
            i = m * (rows // TILE) + r
            for n in range(cols // TILE):
                block = product[r * TILE:(r + 1) * TILE, n * TILE:(n + 1) * TILE]
                block = block * block * keep_ref[i, n].astype(jnp.float32)
                pruned_ref[i * TILE:(i + 1) * TILE, n * TILE:(n + 1) * TILE] = block
                total = total + block
            total_ref[i:i + 1, :] = jnp.sum(total.T, axis=0, keepdims=True)


def normalize(width, pruned_ref, shares_ref, flow_ref, held, sem):
    factors = width / (jnp.sum(shares_ref[...], axis=0, keepdims=True) + 1e-06)
    copies = []
    for i in range(held.shape[0] // TILE):
        at = slice(i * TILE, (i + 1) * TILE)
        factor = jnp.broadcast_to(factors[:, at], (TILE, TILE)).T
        for n in range(held.shape[1] // TILE):
            to = (at, slice(n * TILE, (n + 1) * TILE))
            held[to] = pruned_ref[to] * factor
        copies.append(pltpu.make_async_copy(held.at[pl.ds(i * TILE, TILE)], flow_ref.at[pl.ds(i * TILE, TILE)], sem))
        copies[-1].start()
    for copy in copies:
        copy.wait()


def per_device(left_vals, left_scale, left_keep, right_vals, right_scale, right_keep, result_keep):
    at = jnp.stack([lax.axis_index(a) for a in AXES]).astype(jnp.int32)
    rows, cols = left_vals.shape[0], right_vals.shape[1]
    right_tiles, left_tiles = tiled(
        right_scale, right_keep, right_vals, left_scale.reshape(1, -1), left_keep.reshape(1, -1), left_vals
    )
    z0, h0 = right_tiles[None], left_tiles[None]

    high, lane = [h0], [z0]
    for _ in range(SIDE - 1):
        high.append(step(high[-1], "zh"))
        lane.append(step(lane[-1], "zl"))
    lefts, rights = [], []
    for first in (0, 2):
        own = [join(high[first:first + 2])]
        for _ in range(SIDE - 1):
            own.append(step(own[-1], "y"))
        own = join(own)
        lefts.append((own, (first, 2, 1)))
        lefts.append((swap(own), (first, 2, -1)))
    for first in (0, 2):
        blocks = [join(lane[first:first + 2])]
        for _ in range(SIDE - 1):
            blocks.append(step(blocks[-1], "x"))
        rights += blocks if first else [join(blocks)]
    operands = [v for v, _ in lefts] + rights
    pruned, totals = pl.pallas_call(
        functools.partial(multiply, [p for _, p in lefts]),
        out_shape=(
            jax.ShapeDtypeStruct((rows, cols), jnp.float32),
            jax.ShapeDtypeStruct((rows // TILE, TILE), jnp.float32),
        ),
        in_specs=[SMEM, SMEM] + [VMEM] * len(operands),
        out_specs=(VMEM, VMEM),
        scratch_shapes=[
            pltpu.VMEM((2 * SIDE * SIDE, rows, TILE), jnp.bfloat16),
        ],
        compiler_params=pltpu.CompilerParams(vmem_limit_bytes=20 * MIB),
    )(at, result_keep, *operands)
    totals = totals.reshape(rows)
    totals = lax.psum(totals, "core")
    spread = jnp.broadcast_to(totals, (SIDE * SIDE, rows))
    shares = lax.all_to_all(spread, ("zh", "y"), 0, 0)
    width = cols * lax.axis_size("zh") * lax.axis_size("y") * lax.axis_size("core")
    return pl.pallas_call(
        functools.partial(normalize, float(width)),
        out_shape=jax.ShapeDtypeStruct((rows, cols), jnp.float32),
        in_specs=[VMEM, VMEM],
        out_specs=ANY,
        scratch_shapes=[pltpu.VMEM((rows, cols), jnp.float32), pltpu.SemaphoreType.DMA],
        compiler_params=pltpu.CompilerParams(vmem_limit_bytes=8 * MIB),
    )(pruned, shares)


def solution(mesh):
    fine = Mesh(mesh.devices.reshape(SIDE, SIDE, SIDE, SIDE, 2), AXES)
    spec = P(("x", "zl"), ("zh", "y", "core"))
    return jax.shard_map(
        per_device,
        mesh=fine,
        in_specs=(spec,) * 7,
        out_specs=spec,
        check_vma=False,
    )
```

```python
import functools

import jax
import jax.numpy as jnp
from jax import lax
from jax.experimental import pallas as pl
from jax.experimental.pallas import tpu as pltpu
from jax.sharding import Mesh, PartitionSpec as P

AXES = ("x", "zl", "zh", "y", "core")
SIDE = 4
TILE = 128
MIB = 1024 * 1024
VMEM = pl.BlockSpec(memory_space=pltpu.VMEM)
SMEM = pl.BlockSpec(memory_space=pltpu.SMEM)
ANY = pl.BlockSpec(memory_space=pl.ANY)


def step(value, axis, by=1):
    pairs = []
    for i in range(SIDE):
        pairs.append((2 * i, 2 * ((i + by) % SIDE)))
        pairs.append((2 * i + 1, 2 * ((i - by) % SIDE) + 1))
    return lax.ppermute(value, (axis, "core"), pairs)


def swap(value):
    return lax.ppermute(value, "core", [(0, 1), (1, 0)])


def copy_parts(count, *refs):
    at = 0
    for ref in refs[:count]:
        refs[-1][at:at + ref.shape[0]] = ref[...]
        at += ref.shape[0]


def join(parts):
    shape = (sum(p.shape[0] for p in parts),) + parts[0].shape[1:]
    return pl.pallas_call(
        functools.partial(copy_parts, len(parts)),
        out_shape=jax.ShapeDtypeStruct(shape, jnp.bfloat16),
        in_specs=[VMEM] * len(parts),
        out_specs=VMEM,
        compiler_params=pltpu.CompilerParams(vmem_limit_bytes=10 * MIB),
    )(*parts)


def scale_tiles(*refs):
    given, made, held, sems = refs[:6], refs[6:8], refs[8:14], refs[14]
    copies = [pltpu.make_async_copy(given[i], held[i], sems.at[i]) for i in range(6)]
    for copy in copies:
        copy.start()
    for side in range(2):
        for copy in copies[3 * side:3 * side + 3]:
            copy.wait()
        scale_ref, keep_ref, values_ref = held[3 * side:3 * side + 3]
        factors = scale_ref[...] * keep_ref[...].astype(jnp.float32)
        rows, cols = (n // TILE for n in values_ref.shape)
        for i in range(rows):
            for j in range(cols):
                at = (slice(i * TILE, (i + 1) * TILE), slice(j * TILE, (j + 1) * TILE))
                factor = factors[i:i + 1, j:j + 1] if cols > 1 else factors[0:1, i:i + 1]
                made[side][at] = (values_ref[at].astype(jnp.float32) * factor).astype(jnp.bfloat16)


def tiled(*operands):
    return pl.pallas_call(
        scale_tiles,
        out_shape=[jax.ShapeDtypeStruct(operands[i].shape, jnp.bfloat16) for i in (2, 5)],
        in_specs=[pl.BlockSpec(memory_space=pl.ANY)] * 6,
        out_specs=[VMEM] * 2,
        scratch_shapes=[pltpu.VMEM(v.shape, v.dtype) for v in operands] + [pltpu.SemaphoreType.DMA((6,))],
        compiler_params=pltpu.CompilerParams(vmem_limit_bytes=60 * MIB),
    )(*operands)


def multiply(left_at, at_ref, keep_ref, *refs):
    left_refs, right_refs = refs[:len(left_at)], refs[len(left_at):-3]
    pruned_ref, total_ref, left = refs[-3:]
    x, zl, zh, y, core = (at_ref[i] for i in range(5))
    way = 1 - 2 * core

    for ref, (first, lanes, sign) in zip(left_refs, left_at):
        def put(i, carry, ref=ref, first=first, lanes=lanes, sign=sign):
            k, s = first + lax.rem(i, lanes), lax.div(i, lanes)
            across = lax.rem((x - zh + k * sign * way) * way + 4 * SIDE, SIDE)
            along = lax.rem((zl - y + s * sign * way) * way + 4 * SIDE, SIDE)
            block = lax.div(along, 2) * (2 * SIDE) + across * 2 + lax.rem(along, 2)
            left[block * 2 + (core if sign > 0 else 1 - core)] = ref[i]
            return carry

        lax.fori_loop(0, ref.shape[0], put, 0)
    rows, depth, cols = 2 * TILE, right_refs[0].shape[1], right_refs[0].shape[2]
    for m in range(left.shape[1] // rows):
        product, at = None, 0
        for ref in right_refs:
            count = ref.shape[0] * depth // TILE
            lhs = jnp.concatenate([left[k, m * rows:(m + 1) * rows, :] for k in range(at, at + count)], axis=1)
            part = jnp.dot(lhs, ref[...].reshape(-1, cols), preferred_element_type=jnp.float32)
            product = part if product is None else product + part
            at += count
        for r in range(rows // TILE):
            total = jnp.zeros((TILE, TILE), jnp.float32)
            i = m * (rows // TILE) + r
            for n in range(cols // TILE):
                block = product[r * TILE:(r + 1) * TILE, n * TILE:(n + 1) * TILE]
                block = block * block * keep_ref[i, n].astype(jnp.float32)
                pruned_ref[i * TILE:(i + 1) * TILE, n * TILE:(n + 1) * TILE] = block
                total = total + block
            total_ref[i:i + 1, :] = jnp.sum(total.T, axis=0, keepdims=True)


def normalize(width, pruned_ref, shares_ref, flow_ref, held, sem):
    factors = width / (jnp.sum(shares_ref[...], axis=0, keepdims=True) + 1e-06)
    copies = []
    for i in range(held.shape[0] // TILE):
        at = slice(i * TILE, (i + 1) * TILE)
        factor = jnp.broadcast_to(factors[:, at], (TILE, TILE)).T
        for n in range(held.shape[1] // TILE):
            to = (at, slice(n * TILE, (n + 1) * TILE))
            held[to] = pruned_ref[to] * factor
        copies.append(pltpu.make_async_copy(held.at[pl.ds(i * TILE, TILE)], flow_ref.at[pl.ds(i * TILE, TILE)], sem))
        copies[-1].start()
    for copy in copies:
        copy.wait()


def per_device(left_vals, left_scale, left_keep, right_vals, right_scale, right_keep, result_keep):
    at = jnp.stack([lax.axis_index(a) for a in AXES]).astype(jnp.int32)
    rows, cols = left_vals.shape[0], right_vals.shape[1]
    right_tiles, left_tiles = tiled(
        right_scale, right_keep, right_vals, left_scale.reshape(1, -1), left_keep.reshape(1, -1), left_vals
    )
    z0, h0 = right_tiles[None], left_tiles[None]

    high, lane = [h0], [z0]
    for _ in range(SIDE - 1):
        high.append(step(high[-1], "zh"))
        lane.append(step(lane[-1], "zl"))
    lefts, rights = [], []
    for first in (0, 2):
        own = [join(high[first:first + 2])]
        for _ in range(SIDE - 1):
            own.append(step(own[-1], "y"))
        own = join(own)
        lefts.append((own, (first, 2, 1)))
        lefts.append((swap(own), (first, 2, -1)))
    for first in (0, 2):
        blocks = [join(lane[first:first + 2])]
        for _ in range(SIDE - 1):
            blocks.append(step(blocks[-1], "x"))
        rights.append(join(blocks))
    operands = [v for v, _ in lefts] + rights
    pruned, totals = pl.pallas_call(
        functools.partial(multiply, [p for _, p in lefts]),
        out_shape=(
            jax.ShapeDtypeStruct((rows, cols), jnp.float32),
            jax.ShapeDtypeStruct((rows // TILE, TILE), jnp.float32),
        ),
        in_specs=[SMEM, SMEM] + [VMEM] * len(operands),
        out_specs=(VMEM, VMEM),
        scratch_shapes=[
            pltpu.VMEM((2 * SIDE * SIDE, rows, TILE), jnp.bfloat16),
        ],
        compiler_params=pltpu.CompilerParams(vmem_limit_bytes=20 * MIB),
    )(at, result_keep, *operands)
    totals = totals.reshape(rows)
    totals = lax.psum(totals, "core")
    spread = jnp.broadcast_to(totals, (SIDE * SIDE, rows))
    shares = lax.all_to_all(spread, ("zh", "y"), 0, 0)
    width = cols * lax.axis_size("zh") * lax.axis_size("y") * lax.axis_size("core")
    return pl.pallas_call(
        functools.partial(normalize, float(width)),
        out_shape=jax.ShapeDtypeStruct((rows, cols), jnp.float32),
        in_specs=[VMEM, VMEM],
        out_specs=ANY,
        scratch_shapes=[pltpu.VMEM((rows, cols), jnp.float32), pltpu.SemaphoreType.DMA],
        compiler_params=pltpu.CompilerParams(vmem_limit_bytes=8 * MIB),
    )(pruned, shares)


def solution(mesh):
    fine = Mesh(mesh.devices.reshape(SIDE, SIDE, SIDE, SIDE, 2), AXES)
    spec = P(("x", "zl"), ("zh", "y", "core"))
    return jax.shard_map(
        per_device,
        mesh=fine,
        in_specs=(spec,) * 7,
        out_specs=spec,
        check_vma=False,
    )
```
